32 devices in a mesh: groups: 2 (over x), blk: 16 (over z, y, core).
Axes of the slice: x: 2, y: 2, z: 4, core: 2. Of those that a mesh axis runs over, the one named last changes fastest.
Arguments:
- samples: bfloat16 [64, 65536], P(None, ('groups', 'blk')), parts along dimension 1, may hold values from -6 to 6
- centre_index: int32 [32768], P(('groups', 'blk')), parts along dimension 0, may hold values from 0 to 32767, as said below
- probe_signs: int32 [32, 32768], P(None, ('groups', 'blk')), parts along dimension 1, may hold values from 0 to 1
- probe_scale: float32 [32768], P(('groups', 'blk')), parts along dimension 0, may hold values from 0.5 to 5
Outputs:
- product: float32 [32768, 32], P(('groups', 'blk')), parts along dimension 0
The draws below stay inside these ranges and needn't reach their ends.
There are 2 independent parts, one for each index of `groups`. The reference program is written for one: setup_inputs(seed, part) draws one part's arguments, and reference() takes and returns one part's arrays. A program takes and returns all parts, laid end to end along the dimension named above; each array names one. Nothing has to cross between parts.
Inputs may be any that keep to these rules, and one draw needn't show every extreme that they name: `centre_index`: entry j names the sample serving as centre j. Within each aligned block of 1024 entries, at most 128 name samples of any one aligned block of 2048 samples, and in every such block of entries some block of samples is named exactly 128 times.
All inputs are finite; a program needn't handle non-finite values.
Results may differ from the reference program's by a relative error of at most 0.0031.
Values may be sent and summed in bfloat16 or wider, within the bound.
A program may use at most 64 MiB of HBM per device.

```python
import math
import jax
import jax.numpy as jnp
from jax import lax

F = 64
M = 16384
P_SIZE = 32
S_DEV = 2048
SAMPLES = 32768
M_DEV = 1024
CAP = 128


def draw_centre_index(key, part):
    key = jax.random.fold_in(key, 17)
    owners = SAMPLES // S_DEV
    halves = owners // 2
    keys = jax.random.split(key, 4)
    order = jax.vmap(lambda single: jax.random.permutation(single, owners))(jax.random.split(keys[0], owners))
    share = jax.random.randint(keys[1], (owners, halves), 0, CAP + 1)
    share = share.at[:, 0].set(CAP)
    targets = jnp.arange(owners)
    first = (order[:, 0::2, None] == targets[None, None, :]).astype(jnp.int32)
    second = (order[:, 1::2, None] == targets[None, None, :]).astype(jnp.int32)
    counts = jnp.sum(share[:, :, None] * first + (CAP - share)[:, :, None] * second, axis=1)
    bounds = jnp.cumsum(counts, axis=1)
    slots = jnp.arange(M_DEV)
    owner = jnp.sum((bounds[:, None, :] <= slots[None, :, None]).astype(jnp.int32), axis=2)
    rows = jax.random.randint(keys[2], (owners, M_DEV), 0, S_DEV)
    picked = owner * S_DEV + rows
    shuffle = jax.vmap(lambda single: jax.random.permutation(single, M_DEV))(jax.random.split(keys[3], owners))
    picked = jnp.take_along_axis(picked, shuffle, axis=1)
    return picked.reshape(-1).astype(jnp.int32)


def with_ends(array, own_key, least, top_value):
    longest = array.shape.index(max(array.shape))
    spots = []
    for shift in (0, 1):
        where = [jax.random.randint(jax.random.fold_in(own_key, axis), (), 0, length) for axis, length in enumerate(array.shape)]
        where[longest] = (where[longest] + shift) % array.shape[longest]
        spots.append(tuple(where))
    return array.at[spots[0]].set(least).at[spots[1]].set(top_value)


def block_levels(stream_key, extent, pieces, low, largest):
    level = 1.0
    for axis_at, blocks in pieces:
        heights = jax.random.uniform(jax.random.fold_in(jax.random.fold_in(stream_key, 6), axis_at), (blocks,), jnp.float32, low / len(pieces), largest / len(pieces))
        level = level * jnp.repeat(jnp.exp(heights), extent[axis_at] // blocks).reshape((-1,) + (1,) * (len(extent) - 1 - axis_at))
    return level


def noise(key, shape, spread, most, cuts=(), dtype=jnp.bfloat16):
    loudness = block_levels(key, shape, cuts, -0.22, 0.18) if cuts else 1.0
    result = jax.random.normal(key, shape, jnp.float32) * spread * loudness
    return jnp.minimum(jnp.maximum(result, -most), most).astype(dtype)


def setup_inputs(seed: int = 0, part: int = 0) -> dict:
    arg_keys = jax.random.split(jax.random.key(seed), 5)
    part_keys = jax.random.split(jax.random.fold_in(arg_keys[4], part), 5)
    return {
        "samples": noise(part_keys[0], (F, SAMPLES), 1.0, 6.0, ((1, 16),)),
        "centre_index": draw_centre_index(jax.random.fold_in(jax.random.fold_in(arg_keys[4], part), 71), part),
        "probe_signs": with_ends(jax.random.randint(part_keys[2], (P_SIZE, M), 0, 2), jax.random.fold_in(part_keys[2], 1), 0, 1).astype(jnp.int32),
        "probe_scale": jnp.clip(jnp.exp(math.log(5.0) - 2.3025851 * jax.random.uniform(part_keys[3], (M,), jnp.float32) ** block_levels(part_keys[3], (M,), ((0, 16),), -0.2, 0.2)), 0.5, 5.0),
    }


def kernel_block(points, point_sq, centres):
    centre_sq = jnp.sum(jnp.square(centres.astype(jnp.float32)), axis=0)
    cross = lax.dot_general(points, centres, (((0,), (0,)), ((), ())), preferred_element_type=jnp.float32)
    distance = point_sq[:, None] + centre_sq[None, :] - 2.0 * cross
    return jnp.exp(distance * (-2.0 / F)).astype(jnp.bfloat16)


def reference(samples, centre_index, probe_signs, probe_scale):
    centres = jnp.take(samples, centre_index, axis=1)
    probe = ((2 * probe_signs - 1).astype(jnp.float32) * probe_scale[None, :]).astype(jnp.bfloat16)
    point_sq = jnp.sum(jnp.square(samples.astype(jnp.float32)), axis=0)
    count = SAMPLES // S_DEV
    sample_blocks = jnp.moveaxis(samples.reshape(F, count, S_DEV), 1, 0)
    sq_blocks = point_sq.reshape(count, S_DEV)

    def first(inputs):
        points, squares = inputs
        kernel = kernel_block(points, squares, centres)
        hidden = lax.dot_general(probe, kernel, (((1,), (1,)), ((), ())), preferred_element_type=jnp.float32)
        return hidden.astype(jnp.bfloat16)

    hidden_blocks = lax.map(first, (sample_blocks, sq_blocks))

    def second(total, inputs):
        points, squares, hidden = inputs
        kernel = kernel_block(points, squares, centres)
        term = lax.dot_general(kernel, hidden, (((0,), (1,)), ((), ())), preferred_element_type=jnp.float32)
        return total + term, None

    total, _ = lax.scan(second, jnp.zeros((M, P_SIZE), jnp.float32), (sample_blocks, sq_blocks, hidden_blocks))
    return total / SAMPLES
```

```python
import functools
import math

import jax
import jax.numpy as jnp
from jax import lax
from jax.experimental import pallas as pl
from jax.experimental.pallas import tpu as pltpu
from jax.sharding import PartitionSpec as P

LANES = 128
ROWS = 256
DEPTH = 256
STORE_BYTES = 40 * 2**20
LOG2E = math.log2(math.e)


def three_parts(value):
    high = value.astype(jnp.bfloat16)
    rest = value - high.astype(jnp.float32)
    middle = rest.astype(jnp.bfloat16)
    low = (rest - middle.astype(jnp.float32)).astype(jnp.bfloat16)
    return high, middle, low


def stack_rows(count, rows, columns):
    place = lax.broadcasted_iota(jnp.int32, (count, columns), 0)
    total = jnp.zeros((count, columns), jnp.float32)
    for at, row in enumerate(rows):
        total = jnp.where(place == at, jnp.broadcast_to(row, (count, columns)), total)
    return total


def body(
    blocks, stored, samples, index, signs, scale, out,
    xaug, caug, probe_t, hidden_t, hidden, slot_hot, wanted, asked, reply, arrived,
    pieces, kept, partial, incoming, own,
    ask_send, ask_recv, reply_send, reply_recv, piece_send, piece_recv, sum_send, sum_recv,
):
    features, s_dev = samples.shape
    m_dev = index.shape[1]
    probes = signs.shape[0]
    lines = blocks // 4
    me = lax.axis_index("blk")
    line, side, core = me // 4, (me // 2) % 2, me % 2
    f32, bf16 = jnp.float32, jnp.bfloat16

    def copy_to(peer, src, dst, send, recv):
        return pltpu.make_async_remote_copy(
            src_ref=src, dst_ref=dst, send_sem=send, recv_sem=recv,
            device_id={"blk": peer}, device_id_type=pl.DeviceIdType.MESH,
        )

    barrier = pltpu.get_barrier_semaphore()

    @pl.loop(1, blocks)
    def _(t):
        pl.semaphore_signal(
            barrier, inc=1, device_id={"blk": lax.rem(me + t, blocks)},
            device_id_type=pl.DeviceIdType.MESH,
        )

    picked = index[...]
    owner = picked // s_dev
    place = picked - owner * s_dev
    owner_hot = lax.broadcasted_iota(jnp.int32, (blocks, m_dev), 0) == owner
    owner_bf = jnp.where(owner_hot, 1.0, 0.0).astype(bf16)
    step = min(256, m_dev)
    ranks = []
    for at in range(0, m_dev, step):
        before = lax.broadcasted_iota(jnp.int32, (m_dev, step), 0) < (
            lax.broadcasted_iota(jnp.int32, (m_dev, step), 1) + at
        )
        ranks.append(
            jnp.dot(owner_bf, jnp.where(before, 1.0, 0.0).astype(bf16), preferred_element_type=f32)
        )
    rank = jnp.sum(
        jnp.where(owner_hot, jnp.concatenate(ranks, axis=1), 0.0), axis=0, keepdims=True
    )
    slot = owner * LANES + rank.astype(jnp.int32)
    digits = stack_rows(
        16, [(place // 64).astype(f32), (place % 64).astype(f32)], m_dev
    ).astype(bf16)

    def ask(peer):
        rows = pl.ds(pl.multiple_of(peer * LANES, LANES), LANES)
        hot = lax.broadcasted_iota(jnp.int32, (LANES, m_dev), 0) + peer * LANES == slot
        hot = jnp.where(hot, 1.0, 0.0).astype(bf16)
        slot_hot[rows, :] = hot
        found = lax.dot_general(digits, hot, (((1,), (1,)), ((), ())), preferred_element_type=f32)
        return jnp.broadcast_to(found[0:1] * 64.0 + found[1:2], (8, LANES))

    asked[me] = ask(me)
    pl.semaphore_wait(barrier, blocks - 1)

    @pl.loop(1, blocks)
    def _(t):
        peer = lax.rem(me + t, blocks)
        wanted[peer] = ask(peer)
        copy_to(peer, wanted.at[peer], asked.at[me], ask_send.at[peer], ask_recv.at[me]).start()

    ones = jnp.ones((1, s_dev), f32)
    points = samples[...]
    wide = points.astype(f32)
    norm = jnp.sum(wide * wide, axis=0, keepdims=True) * (-2.0 * LOG2E / features)
    parts = [part.astype(f32) for part in three_parts(norm)]
    turned = wide.T.astype(bf16)
    for at in range(3):
        xaug[:, at * features:(at + 1) * features] = turned
    rest = DEPTH - 3 * features
    xaug[:, 3 * features:] = stack_rows(rest, parts + [ones] * 3, s_dev).T.astype(bf16)
    hidden_t[...] = jnp.zeros_like(hidden_t)

    def answer(peer):
        want = asked[peer][0:1].astype(jnp.int32)
        hot = lax.broadcasted_iota(jnp.int32, (s_dev, LANES), 0) == want
        hot = jnp.where(hot, 1.0, 0.0).astype(bf16)
        return jnp.dot(points, hot, preferred_element_type=f32).astype(bf16)

    mine = pl.ds(pl.multiple_of(me * LANES, LANES), LANES)
    arrived[:, mine] = answer(me)

    @pl.loop(1, blocks)
    def _(t):
        peer = lax.rem(me - t + blocks, blocks)
        copy_to(peer, wanted.at[peer], asked.at[peer], ask_send.at[peer], ask_recv.at[peer]).wait_recv()
        reply[peer] = answer(peer)
        copy_to(
            peer, reply.at[peer], arrived.at[:, mine], reply_send.at[peer], reply_recv.at[me]
        ).start()

    probe = (2 * signs[...] - 1).astype(f32) * scale[...]
    pieces[me, features:, :] = probe.astype(bf16)

    @pl.loop(1, blocks)
    def _(t):
        peer = lax.rem(me + t, blocks)
        theirs = pl.ds(pl.multiple_of(peer * LANES, LANES), LANES)
        copy_to(
            peer, reply.at[peer], arrived.at[:, theirs], reply_send.at[peer], reply_recv.at[peer]
        ).wait_recv()

    pieces[me, :features, :] = jnp.dot(
        arrived[...], slot_hot[...], preferred_element_type=f32
    ).astype(bf16)

    def holder(back, flip_side, flip_core):
        return (
            lax.rem(line - back + lines, lines) * 4
            + lax.rem(side + flip_side, 2) * 2
            + lax.rem(core + flip_core, 2)
        )

    def send_piece(piece, peer, at):
        return copy_to(
            peer, pieces.at[piece], pieces.at[piece], piece_send.at[at], piece_recv.at[piece]
        )

    def prepare(piece):
        c = pieces[piece, :features, :].astype(f32)
        for at, part in enumerate(three_parts(c * (4.0 * LOG2E / features))):
            caug[at * features:(at + 1) * features, :] = part
        square = jnp.sum(c * c, axis=0, keepdims=True) * (-2.0 * LOG2E / features)
        parts = [part.astype(f32) for part in three_parts(square)]
        ones = jnp.ones((1, m_dev), f32)
        caug[3 * features:, :] = stack_rows(rest, [ones] * 3 + parts, m_dev).astype(bf16)

    def kernel_rows(rows):
        power = jnp.dot(xaug[rows, :], caug[...], preferred_element_type=f32)
        return jnp.exp2(power).astype(bf16)

    def first(piece, at):
        prepare(piece)
        probe_t[...] = pieces[piece, features:, :].astype(f32).T.astype(bf16)

        @pl.loop(0, s_dev // ROWS)
        def _(tile):
            rows = pl.ds(pl.multiple_of(tile * ROWS, ROWS), ROWS)
            kernel = kernel_rows(rows)

            @pl.when(at < stored)
            def _():
                kept[lax.rem(at, stored), rows, :] = kernel

            hidden_t[rows, :] += jnp.dot(kernel, probe_t[...], preferred_element_type=f32)

    @pl.loop(0, lines)
    def _(back):
        held = holder(back, 0, 0)

        @pl.when(back > 0)
        def _():
            send_piece(held, held, 0).wait_recv()

        @pl.when(back < lines - 1)
        def _():
            send_piece(held, holder(lines - 1, 0, 0), back * 4).start()

        send_piece(held, holder(0, 1, 0), back * 4 + 1).start()
        send_piece(held, holder(0, 0, 1), back * 4 + 2).start()
        first(held, back * 4)
        near = holder(back, 0, 1)
        send_piece(near, near, 0).wait_recv()
        first(near, back * 4 + 1)
        across = holder(back, 1, 0)
        send_piece(across, across, 0).wait_recv()
        send_piece(across, holder(0, 0, 1), back * 4 + 3).start()
        first(across, back * 4 + 2)
        last = holder(back, 1, 1)
        send_piece(last, last, 0).wait_recv()
        first(last, back * 4 + 3)

    hidden[...] = hidden_t[...].T.astype(bf16)

    def second(at):
        def from_store():
            return jnp.dot(hidden[...], kept[at], preferred_element_type=f32)

        return from_store()

    def holder_at(at):
        return holder(at // 4, lax.rem(at // 2, 2), lax.rem(at, 2))

    def send_sum(peer):
        copy_to(peer, partial.at[peer], incoming.at[me], sum_send.at[peer], sum_recv.at[me]).start()

    @pl.loop(0, blocks - stored)
    def _(t):
        peer = holder_at(blocks - 1 - t)
        prepare(peer)
        own[...] = jnp.zeros_like(own)

        @pl.loop(0, s_dev // ROWS)
        def _(tile):
            rows = pl.ds(pl.multiple_of(tile * ROWS, ROWS), ROWS)
            own[...] += jnp.dot(hidden[:, rows], kernel_rows(rows), preferred_element_type=f32)

        partial[peer] = own[...].astype(bf16)
        send_sum(peer)

    @pl.loop(0, stored - 1)
    def _(t):
        at = stored - 1 - t
        peer = holder_at(at)
        partial[peer] = second(at).astype(bf16)
        send_sum(peer)

    own[...] = second(0)

    @pl.loop(1, blocks)
    def _(t):
        peer = lax.rem(me + t, blocks)
        copy_to(peer, partial.at[peer], incoming.at[peer], sum_send.at[peer], sum_recv.at[peer]).wait()
        own[...] += incoming[peer].astype(f32)

    out[...] = (own[...] * (1.0 / (s_dev * blocks))).T

    @pl.loop(1, blocks)
    def _(t):
        peer = lax.rem(me + t, blocks)
        copy_to(peer, wanted.at[peer], asked.at[peer], ask_send.at[peer], ask_recv.at[peer]).wait_send()
        copy_to(
            peer, reply.at[peer], arrived.at[:, mine], reply_send.at[peer], reply_recv.at[peer]
        ).wait_send()

    @pl.loop(0, lines)
    def _(back):
        @pl.when(back < lines - 1)
        def _():
            send_piece(me, holder(lines - 1, 0, 0), back * 4).wait_send()

        send_piece(me, holder(0, 1, 0), back * 4 + 1).wait_send()
        send_piece(me, holder(0, 0, 1), back * 4 + 2).wait_send()
        send_piece(me, holder(0, 0, 1), back * 4 + 3).wait_send()


def local(samples, centre_index, probe_signs, probe_scale):
    blocks = lax.axis_size("blk")
    features, s_dev = samples.shape
    m_dev = centre_index.shape[0]
    probes = probe_signs.shape[0]
    f32, bf16 = jnp.float32, jnp.bfloat16
    stored = min(blocks, STORE_BYTES // (s_dev * m_dev * 2))
    vmem = pl.BlockSpec(memory_space=pltpu.VMEM)
    return pl.pallas_call(
        functools.partial(body, blocks, stored),
        out_shape=jax.ShapeDtypeStruct((m_dev, probes), f32),
        in_specs=[vmem] * 4,
        out_specs=vmem,
        scratch_shapes=[
            pltpu.VMEM((s_dev, DEPTH), bf16),
            pltpu.VMEM((DEPTH, m_dev), bf16),
            pltpu.VMEM((m_dev, probes), bf16),
            pltpu.VMEM((s_dev, probes), f32),
            pltpu.VMEM((probes, s_dev), bf16),
            pltpu.VMEM((blocks * LANES, m_dev), bf16),
            pltpu.VMEM((blocks, 8, LANES), f32),
            pltpu.VMEM((blocks, 8, LANES), f32),
            pltpu.VMEM((blocks, features, LANES), bf16),
            pltpu.VMEM((features, blocks * LANES), bf16),
            pltpu.VMEM((blocks, features + probes, m_dev), bf16),
            pltpu.VMEM((stored, s_dev, m_dev), bf16),
            pltpu.VMEM((blocks, probes, m_dev), bf16),
            pltpu.VMEM((blocks, probes, m_dev), bf16),
            pltpu.VMEM((probes, m_dev), f32),
        ] + [pltpu.SemaphoreType.DMA((blocks,))] * 8,
        compiler_params=pltpu.CompilerParams(
            collective_id=0, has_side_effects=True, vmem_limit_bytes=62 * 2**20
        ),
    )(samples, centre_index[None, :], probe_signs, probe_scale[None, :])


def solution(mesh):
    in_specs = (
        P(None, ("groups", "blk")),
        P(("groups", "blk")),
        P(None, ("groups", "blk")),
        P(("groups", "blk")),
    )
    out_specs = P(("groups", "blk"), None)
    return jax.shard_map(local, mesh=mesh, in_specs=in_specs, out_specs=out_specs, check_vma=False)
```

```python
import functools
import math

import jax
import jax.numpy as jnp
from jax import lax
from jax.experimental import pallas as pl
from jax.experimental.pallas import tpu as pltpu
from jax.sharding import PartitionSpec as P

LANES = 128
ROWS = 2048
DEPTH = 256
STORE_BYTES = 32 * 2**20
LOG2E = math.log2(math.e)


def three_parts(value):
    high = value.astype(jnp.bfloat16)
    rest = value - high.astype(jnp.float32)
    middle = rest.astype(jnp.bfloat16)
    low = (rest - middle.astype(jnp.float32)).astype(jnp.bfloat16)
    return high, middle, low


def stack_rows(count, rows, columns):
    place = lax.broadcasted_iota(jnp.int32, (count, columns), 0)
    total = jnp.zeros((count, columns), jnp.float32)
    for at, row in enumerate(rows):
        total = jnp.where(place == at, jnp.broadcast_to(row, (count, columns)), total)
    return total


def body(
    blocks, stored, samples, index, signs, scale, out,
    xaug, caug, hidden_t, hidden, slot_hot, wanted, asked, reply, arrived,
    pieces, kept, partial, from_twin, incoming, own,
    ask_send, ask_recv, reply_send, reply_recv, piece_send, piece_recv,
    twin_send, twin_recv, sum_send, sum_recv,
):
    features, s_dev = samples.shape
    m_dev = index.shape[1]
    probes = signs.shape[0]
    lines = blocks // 4
    me = lax.axis_index("blk")
    line, side, core = me // 4, (me // 2) % 2, me % 2
    f32, bf16 = jnp.float32, jnp.bfloat16
    if blocks * LANES == s_dev:
        slot_hot = kept.at[stored]

    def copy_to(peer, src, dst, send, recv):
        return pltpu.make_async_remote_copy(
            src_ref=src, dst_ref=dst, send_sem=send, recv_sem=recv,
            device_id={"blk": peer}, device_id_type=pl.DeviceIdType.MESH,
        )

    barrier = pltpu.get_barrier_semaphore()

    @pl.loop(1, blocks)
    def _(t):
        pl.semaphore_signal(
            barrier, inc=1, device_id={"blk": lax.rem(me + t, blocks)},
            device_id_type=pl.DeviceIdType.MESH,
        )

    picked = index[...]
    owner = picked // s_dev
    place = picked - owner * s_dev
    owner_hot = lax.broadcasted_iota(jnp.int32, (blocks, m_dev), 0) == owner
    owner_bf = jnp.where(owner_hot, 1.0, 0.0).astype(bf16)
    step = min(256, m_dev)
    ranks = []
    for at in range(0, m_dev, step):
        before = lax.broadcasted_iota(jnp.int32, (m_dev, step), 0) < (
            lax.broadcasted_iota(jnp.int32, (m_dev, step), 1) + at
        )
        ranks.append(
            jnp.dot(owner_bf, jnp.where(before, 1.0, 0.0).astype(bf16), preferred_element_type=f32)
        )
    rank = jnp.sum(
        jnp.where(owner_hot, jnp.concatenate(ranks, axis=1), 0.0), axis=0, keepdims=True
    )
    slot = owner * LANES + rank.astype(jnp.int32)
    digits = stack_rows(
        16, [(place // 64).astype(f32), (place % 64).astype(f32)], m_dev
    ).astype(bf16)

    def ask(peer):
        rows = pl.ds(pl.multiple_of(peer * LANES, LANES), LANES)
        hot = lax.broadcasted_iota(jnp.int32, (LANES, m_dev), 0) + peer * LANES == slot
        hot = jnp.where(hot, 1.0, 0.0).astype(bf16)
        slot_hot[rows, :] = hot
        found = lax.dot_general(digits, hot, (((1,), (1,)), ((), ())), preferred_element_type=f32)
        return jnp.broadcast_to(found[0:1] * 64.0 + found[1:2], (8, LANES))

    asked[me] = ask(me)
    pl.semaphore_wait(barrier, blocks - 1)

    @pl.loop(1, blocks)
    def _(t):
        peer = lax.rem(me + t, blocks)
        wanted[peer] = ask(peer)
        copy_to(peer, wanted.at[peer], asked.at[me], ask_send.at[peer], ask_recv.at[me]).start()

    ones = jnp.ones((1, s_dev), f32)
    points = samples[...]
    wide = points.astype(f32)
    norm = jnp.sum(wide * wide, axis=0, keepdims=True) * (-2.0 * LOG2E / features)
    parts = [part.astype(f32) for part in three_parts(norm)]
    turned = wide.T.astype(bf16)
    for at in range(3):
        xaug[:, at * features:(at + 1) * features] = turned
    rest = DEPTH - 3 * features
    xaug[:, 3 * features:] = stack_rows(rest, parts + [ones] * 3, s_dev).T.astype(bf16)
    hidden_t[...] = jnp.zeros_like(hidden_t)

    def answer(peer):
        want = asked[peer][0:1].astype(jnp.int32)
        hot = lax.broadcasted_iota(jnp.int32, (s_dev, LANES), 0) == want
        hot = jnp.where(hot, 1.0, 0.0).astype(bf16)
        return jnp.dot(points, hot, preferred_element_type=f32).astype(bf16)

    mine = pl.ds(pl.multiple_of(me * LANES, LANES), LANES)
    arrived[:, mine] = answer(me)

    @pl.loop(1, blocks)
    def _(t):
        peer = lax.rem(me - t + blocks, blocks)
        copy_to(peer, wanted.at[peer], asked.at[peer], ask_send.at[peer], ask_recv.at[peer]).wait_recv()
        reply[peer] = answer(peer)
        copy_to(
            peer, reply.at[peer], arrived.at[:, mine], reply_send.at[peer], reply_recv.at[me]
        ).start()

    probe = (2 * signs[...] - 1).astype(f32) * scale[...]
    pieces[me, features:, :] = probe.astype(bf16)

    @pl.loop(1, blocks)
    def _(t):
        peer = lax.rem(me + t, blocks)
        theirs = pl.ds(pl.multiple_of(peer * LANES, LANES), LANES)
        copy_to(
            peer, reply.at[peer], arrived.at[:, theirs], reply_send.at[peer], reply_recv.at[peer]
        ).wait_recv()

    pieces[me, :features, :] = jnp.dot(
        arrived[...], slot_hot[...], preferred_element_type=f32
    ).astype(bf16)

    def holder(back, flip_side, flip_core):
        return (
            lax.rem(line - back + lines, lines) * 4
            + lax.rem(side + flip_side, 2) * 2
            + lax.rem(core + flip_core, 2)
        )

    def send_piece(piece, peer, at):
        return copy_to(
            peer, pieces.at[piece], pieces.at[piece], piece_send.at[at], piece_recv.at[piece]
        )

    def prepare(piece):
        c = pieces[piece, :features, :].astype(f32)
        for at, part in enumerate(three_parts(c * (4.0 * LOG2E / features))):
            caug[at * features:(at + 1) * features, :] = part
        square = jnp.sum(c * c, axis=0, keepdims=True) * (-2.0 * LOG2E / features)
        parts = [part.astype(f32) for part in three_parts(square)]
        ones = jnp.ones((1, m_dev), f32)
        caug[3 * features:, :] = stack_rows(rest, [ones] * 3 + parts, m_dev).astype(bf16)

    def kernel_rows(rows):
        power = jnp.dot(xaug[rows, :], caug[...], preferred_element_type=f32)
        return jnp.exp2(power).astype(bf16)

    def first(piece, at):
        prepare(piece)

        @pl.loop(0, s_dev // ROWS)
        def _(tile):
            rows = pl.ds(pl.multiple_of(tile * ROWS, ROWS), ROWS)
            kernel = kernel_rows(rows)

            kept[lax.min(at, stored), rows, :] = kernel
            hidden_t[:, rows] += lax.dot_general(
                pieces[piece, features:, :], kernel, (((1,), (1,)), ((), ())),
                preferred_element_type=f32,
            )

    @pl.loop(0, lines)
    def _(back):
        held = holder(back, 0, 0)

        @pl.when(back > 0)
        def _():
            send_piece(held, held, 0).wait_recv()

        @pl.when(back < lines - 1)
        def _():
            send_piece(held, holder(lines - 1, 0, 0), back * 4).start()

        send_piece(held, holder(0, 1, 0), back * 4 + 1).start()
        send_piece(held, holder(0, 0, 1), back * 4 + 2).start()
        first(held, back * 4)
        near = holder(back, 0, 1)
        send_piece(near, near, 0).wait_recv()
        first(near, back * 4 + 1)
        across = holder(back, 1, 0)
        send_piece(across, across, 0).wait_recv()
        send_piece(across, holder(0, 0, 1), back * 4 + 3).start()
        first(across, back * 4 + 2)
        last = holder(back, 1, 1)
        send_piece(last, last, 0).wait_recv()
        first(last, back * 4 + 3)

    hidden[...] = hidden_t[...].astype(bf16)

    def holder_at(at):
        return holder(at // 4, lax.rem(at // 2, 2), lax.rem(at, 2))

    twin = holder(0, 0, 1)

    def send_twin(pair):
        return copy_to(
            twin, partial.at[2 * pair + 1], from_twin.at[pair],
            twin_send.at[pair], twin_recv.at[pair],
        )

    def send_sum(pair, peer, slot):
        return copy_to(
            peer, partial.at[2 * pair], incoming.at[slot], sum_send.at[pair], sum_recv.at[slot]
        )

    def both(pair, product):
        partial[2 * pair + 1] = product(2 * pair + 1).astype(bf16)
        send_twin(pair).start()
        total = product(2 * pair)
        send_twin(pair).wait_recv()
        return total + from_twin[pair].astype(f32)

    def forward(pair, total):
        partial[2 * pair] = total.astype(bf16)
        send_sum(pair, holder_at(2 * pair), me // 2).start()

    def again(at):
        prepare(holder_at(at))
        own[...] = jnp.zeros_like(own)

        @pl.loop(0, s_dev // ROWS)
        def _(tile):
            rows = pl.ds(pl.multiple_of(tile * ROWS, ROWS), ROWS)
            own[...] += jnp.dot(hidden[:, rows], kernel_rows(rows), preferred_element_type=f32)

        return own[...]

    def from_store(at):
        return jnp.dot(hidden[...], kept[at], preferred_element_type=f32)

    pairs, stored_pairs = blocks // 2, stored // 2

    @pl.loop(0, pairs - stored_pairs)
    def _(t):
        pair = pairs - 1 - t
        forward(pair, both(pair, again))

    @pl.loop(0, stored_pairs - 1)
    def _(t):
        pair = stored_pairs - 1 - t
        forward(pair, both(pair, from_store))

    own[...] = both(0, from_store)

    @pl.loop(1, pairs)
    def _(pair):
        slot = holder_at(2 * pair) // 2
        send_sum(pair, me, slot).wait_recv()
        own[...] += incoming[slot].astype(f32)

    out[...] = (own[...] * (1.0 / (s_dev * blocks))).T

    @pl.loop(1, blocks)
    def _(t):
        peer = lax.rem(me + t, blocks)
        copy_to(peer, wanted.at[peer], asked.at[peer], ask_send.at[peer], ask_recv.at[peer]).wait_send()
        copy_to(
            peer, reply.at[peer], arrived.at[:, mine], reply_send.at[peer], reply_recv.at[peer]
        ).wait_send()

    send_twin(0).wait_send()

    @pl.loop(1, pairs)
    def _(pair):
        send_twin(pair).wait_send()
        send_sum(pair, me, pair).wait_send()

    @pl.loop(0, lines)
    def _(back):
        @pl.when(back < lines - 1)
        def _():
            send_piece(me, holder(lines - 1, 0, 0), back * 4).wait_send()

        send_piece(me, holder(0, 1, 0), back * 4 + 1).wait_send()
        send_piece(me, holder(0, 0, 1), back * 4 + 2).wait_send()
        send_piece(me, holder(0, 0, 1), back * 4 + 3).wait_send()


def local(samples, centre_index, probe_signs, probe_scale):
    blocks = lax.axis_size("blk")
    features, s_dev = samples.shape
    m_dev = centre_index.shape[0]
    probes = probe_signs.shape[0]
    f32, bf16 = jnp.float32, jnp.bfloat16
    stored = min(blocks, STORE_BYTES // (s_dev * m_dev * 2)) // 2 * 2
    vmem = pl.BlockSpec(memory_space=pltpu.VMEM)
    return pl.pallas_call(
        functools.partial(body, blocks, stored),
        out_shape=jax.ShapeDtypeStruct((m_dev, probes), f32),
        in_specs=[vmem] * 4,
        out_specs=vmem,
        scratch_shapes=[
            pltpu.VMEM((s_dev, DEPTH), bf16),
            pltpu.VMEM((DEPTH, m_dev), bf16),
            pltpu.VMEM((probes, s_dev), f32),
            pltpu.VMEM((probes, s_dev), bf16),
            pltpu.VMEM((16 if blocks * LANES == s_dev else blocks * LANES, m_dev), bf16),
            pltpu.VMEM((blocks, 8, LANES), f32),
            pltpu.VMEM((blocks, 8, LANES), f32),
            pltpu.VMEM((blocks, features, LANES), bf16),
            pltpu.VMEM((features, blocks * LANES), bf16),
            pltpu.VMEM((blocks, features + probes, m_dev), bf16),
            pltpu.VMEM((stored + 1, s_dev, m_dev), bf16),
            pltpu.VMEM((blocks, probes, m_dev), bf16),
            pltpu.VMEM((blocks // 2, probes, m_dev), bf16),
            pltpu.VMEM((blocks // 2, probes, m_dev), bf16),
            pltpu.VMEM((probes, m_dev), f32),
        ] + [pltpu.SemaphoreType.DMA((blocks,))] * 10,
        compiler_params=pltpu.CompilerParams(
            collective_id=0, has_side_effects=True, vmem_limit_bytes=62 * 2**20
        ),
    )(samples, centre_index[None, :], probe_signs, probe_scale[None, :])


def solution(mesh):
    in_specs = (
        P(None, ("groups", "blk")),
        P(("groups", "blk")),
        P(None, ("groups", "blk")),
        P(("groups", "blk")),
    )
    out_specs = P(("groups", "blk"), None)
    return jax.shard_map(local, mesh=mesh, in_specs=in_specs, out_specs=out_specs, check_vma=False)
```

```python
import functools
import math

import jax
import jax.numpy as jnp
from jax import lax
from jax.experimental import pallas as pl
from jax.experimental.pallas import tpu as pltpu
from jax.sharding import PartitionSpec as P

LANES = 128
ROWS = 1024
DEPTH = 256
STORE_BYTES = 40 * 2**20
LOG2E = math.log2(math.e)


def three_parts(value):
    high = value.astype(jnp.bfloat16)
    rest = value - high.astype(jnp.float32)
    middle = rest.astype(jnp.bfloat16)
    low = (rest - middle.astype(jnp.float32)).astype(jnp.bfloat16)
    return high, middle, low


def stack_rows(count, rows, columns):
    place = lax.broadcasted_iota(jnp.int32, (count, columns), 0)
    total = jnp.zeros((count, columns), jnp.float32)
    for at, row in enumerate(rows):
        total = jnp.where(place == at, jnp.broadcast_to(row, (count, columns)), total)
    return total


def body(
    blocks, stored, samples, index, signs, scale, out,
    xaug, caug, hidden_t, hidden, slot_hot, wanted, asked, reply, arrived,
    pieces, kept, partial, from_twin, incoming, own,
    ask_send, ask_recv, reply_send, reply_recv, piece_send, piece_recv,
    twin_send, twin_recv, sum_send, sum_recv,
):
    features, s_dev = samples.shape
    m_dev = index.shape[1]
    probes = signs.shape[0]
    lines = blocks // 4
    me = lax.axis_index("blk")
    line, side, core = me // 4, (me // 2) % 2, me % 2
    f32, bf16 = jnp.float32, jnp.bfloat16
    if blocks * LANES == s_dev:
        slot_hot = kept.at[stored]

    def copy_to(peer, src, dst, send, recv):
        return pltpu.make_async_remote_copy(
            src_ref=src, dst_ref=dst, send_sem=send, recv_sem=recv,
            device_id={"blk": peer}, device_id_type=pl.DeviceIdType.MESH,
        )

    barrier = pltpu.get_barrier_semaphore()

    @pl.loop(1, blocks)
    def _(t):
        pl.semaphore_signal(
            barrier, inc=1, device_id={"blk": lax.rem(me + t, blocks)},
            device_id_type=pl.DeviceIdType.MESH,
        )

    picked = index[...]
    owner = picked // s_dev
    place = picked - owner * s_dev
    owner_hot = lax.broadcasted_iota(jnp.int32, (blocks, m_dev), 0) == owner
    owner_bf = jnp.where(owner_hot, 1.0, 0.0).astype(bf16)
    step = min(256, m_dev)
    ranks = []
    for at in range(0, m_dev, step):
        before = lax.broadcasted_iota(jnp.int32, (m_dev, step), 0) < (
            lax.broadcasted_iota(jnp.int32, (m_dev, step), 1) + at
        )
        ranks.append(
            jnp.dot(owner_bf, jnp.where(before, 1.0, 0.0).astype(bf16), preferred_element_type=f32)
        )
    rank = jnp.sum(
        jnp.where(owner_hot, jnp.concatenate(ranks, axis=1), 0.0), axis=0, keepdims=True
    )
    slot = owner * LANES + rank.astype(jnp.int32)
    digits = stack_rows(
        16, [(place // 64).astype(f32), (place % 64).astype(f32)], m_dev
    ).astype(bf16)

    for at in range(0, blocks * LANES, 512):
        hot = lax.broadcasted_iota(jnp.int32, (512, m_dev), 0) + at == slot
        slot_hot[at:at + 512, :] = jnp.where(hot, 1.0, 0.0).astype(bf16)
    found = lax.dot_general(
        digits, slot_hot[...], (((1,), (1,)), ((), ())), preferred_element_type=f32
    )
    found = found[0:1] * 64.0 + found[1:2]
    for peer in range(blocks):
        wanted[peer] = jnp.broadcast_to(found[:, peer * LANES:(peer + 1) * LANES], (8, LANES))
    asked[me] = wanted[me]
    pl.semaphore_wait(barrier, blocks - 1)

    @pl.loop(1, blocks)
    def _(t):
        peer = lax.rem(me + t, blocks)
        copy_to(peer, wanted.at[peer], asked.at[me], ask_send.at[peer], ask_recv.at[me]).start()

    ones = jnp.ones((1, s_dev), f32)
    points = samples[...]
    wide = points.astype(f32)
    norm = jnp.sum(wide * wide, axis=0, keepdims=True) * (-2.0 * LOG2E / features)
    parts = [part.astype(f32) for part in three_parts(norm)]
    turned = wide.T.astype(bf16)
    for at in range(3):
        xaug[:, at * features:(at + 1) * features] = turned
    rest = DEPTH - 3 * features
    xaug[:, 3 * features:] = stack_rows(rest, parts + [ones] * 3, s_dev).T.astype(bf16)
    hidden_t[...] = jnp.zeros_like(hidden_t)

    mine = pl.ds(pl.multiple_of(me * LANES, LANES), LANES)
    group = 4

    @pl.loop(0, blocks // group)
    def _(step):
        peers = [lax.rem(me - step * group - t + blocks, blocks) for t in range(group)]
        for t, peer in enumerate(peers):
            @pl.when(step * group + t > 0)
            def _(peer=peer):
                copy_to(
                    peer, wanted.at[peer], asked.at[peer], ask_send.at[peer], ask_recv.at[peer]
                ).wait_recv()

        want = jnp.concatenate([asked[peer][0:1] for peer in peers], axis=1).astype(jnp.int32)
        hot = lax.broadcasted_iota(jnp.int32, (s_dev, group * LANES), 0) == want
        hot = jnp.where(hot, 1.0, 0.0).astype(bf16)
        chosen = jnp.dot(points, hot, preferred_element_type=f32).astype(bf16)
        for t, peer in enumerate(peers):
            reply[peer] = chosen[:, t * LANES:(t + 1) * LANES]

            @pl.when(step * group + t > 0)
            def _(peer=peer):
                copy_to(
                    peer, reply.at[peer], arrived.at[:, mine],
                    reply_send.at[peer], reply_recv.at[me],
                ).start()

    arrived[:, mine] = reply[me]

    probe = (2 * signs[...] - 1).astype(f32) * scale[...]
    pieces[me, features:, :] = probe.astype(bf16)

    @pl.loop(1, blocks)
    def _(t):
        peer = lax.rem(me + t, blocks)
        theirs = pl.ds(pl.multiple_of(peer * LANES, LANES), LANES)
        copy_to(
            peer, reply.at[peer], arrived.at[:, theirs], reply_send.at[peer], reply_recv.at[peer]
        ).wait_recv()

    pieces[me, :features, :] = jnp.dot(
        arrived[...], slot_hot[...], preferred_element_type=f32
    ).astype(bf16)

    def holder(back, flip_side, flip_core):
        return (
            lax.rem(line - back + lines, lines) * 4
            + lax.rem(side + flip_side, 2) * 2
            + lax.rem(core + flip_core, 2)
        )

    def send_piece(piece, peer, at):
        return copy_to(
            peer, pieces.at[piece], pieces.at[piece], piece_send.at[at], piece_recv.at[piece]
        )

    def prepare(piece):
        c = pieces[piece, :features, :].astype(f32)
        for at, part in enumerate(three_parts(c * (4.0 * LOG2E / features))):
            caug[at * features:(at + 1) * features, :] = part
        square = jnp.sum(c * c, axis=0, keepdims=True) * (-2.0 * LOG2E / features)
        parts = [part.astype(f32) for part in three_parts(square)]
        ones = jnp.ones((1, m_dev), f32)
        caug[3 * features:, :] = stack_rows(rest, [ones] * 3 + parts, m_dev).astype(bf16)

    def kernel_rows(rows):
        power = jnp.dot(xaug[rows, :], caug[...], preferred_element_type=f32)
        return jnp.exp2(power).astype(bf16)

    def first(piece, at):
        prepare(piece)

        @pl.loop(0, s_dev // ROWS, unroll=2)
        def _(tile):
            rows = pl.ds(pl.multiple_of(tile * ROWS, ROWS), ROWS)
            kernel = kernel_rows(rows)

            kept[lax.min(at, stored), rows, :] = kernel
            hidden_t[:, rows] += lax.dot_general(
                pieces[piece, features:, :], kernel, (((1,), (1,)), ((), ())),
                preferred_element_type=f32,
            )

    @pl.loop(0, lines)
    def _(back):
        held = holder(back, 0, 0)

        @pl.when(back > 0)
        def _():
            send_piece(held, held, 0).wait_recv()

        @pl.when(back < lines - 1)
        def _():
            send_piece(held, holder(lines - 1, 0, 0), back * 4).start()

        send_piece(held, holder(0, 1, 0), back * 4 + 1).start()
        send_piece(held, holder(0, 0, 1), back * 4 + 2).start()
        first(held, back * 4)
        near = holder(back, 0, 1)
        send_piece(near, near, 0).wait_recv()
        first(near, back * 4 + 1)
        across = holder(back, 1, 0)
        send_piece(across, across, 0).wait_recv()
        send_piece(across, holder(0, 0, 1), back * 4 + 3).start()
        first(across, back * 4 + 2)
        last = holder(back, 1, 1)
        send_piece(last, last, 0).wait_recv()
        first(last, back * 4 + 3)

    hidden[...] = hidden_t[...].astype(bf16)

    def holder_at(at):
        return holder(at // 4, lax.rem(at // 2, 2), lax.rem(at, 2))

    twin = holder(0, 0, 1)

    def send_twin(pair):
        return copy_to(
            twin, partial.at[2 * pair + 1], from_twin.at[pair],
            twin_send.at[pair], twin_recv.at[pair],
        )

    def send_sum(pair, peer, slot):
        return copy_to(
            peer, partial.at[2 * pair], incoming.at[slot], sum_send.at[pair], sum_recv.at[slot]
        )

    def both(pair, product):
        partial[2 * pair + 1] = product(2 * pair + 1).astype(bf16)
        send_twin(pair).start()
        total = product(2 * pair)
        send_twin(pair).wait_recv()
        return total + from_twin[pair].astype(f32)

    def forward(pair, total):
        partial[2 * pair] = total.astype(bf16)
        send_sum(pair, holder_at(2 * pair), me // 2).start()

    def again(at):
        prepare(holder_at(at))
        own[...] = jnp.zeros_like(own)

        @pl.loop(0, s_dev // ROWS, unroll=2)
        def _(tile):
            rows = pl.ds(pl.multiple_of(tile * ROWS, ROWS), ROWS)
            own[...] += jnp.dot(hidden[:, rows], kernel_rows(rows), preferred_element_type=f32)

        return own[...]

    def from_store(at):
        return jnp.dot(hidden[...], kept[at], preferred_element_type=f32)

    pairs, stored_pairs = blocks // 2, stored // 2

    @pl.loop(0, pairs - stored_pairs)
    def _(t):
        pair = pairs - 1 - t
        forward(pair, both(pair, again))

    @pl.loop(0, stored_pairs - 1)
    def _(t):
        pair = stored_pairs - 1 - t
        forward(pair, both(pair, from_store))

    own[...] = both(0, from_store)

    @pl.loop(1, pairs)
    def _(pair):
        slot = holder_at(2 * pair) // 2
        send_sum(pair, me, slot).wait_recv()
        own[...] += incoming[slot].astype(f32)

    out[...] = own[...] * (1.0 / (s_dev * blocks))

    @pl.loop(1, blocks)
    def _(t):
        peer = lax.rem(me + t, blocks)
        copy_to(peer, wanted.at[peer], asked.at[peer], ask_send.at[peer], ask_recv.at[peer]).wait_send()
        copy_to(
            peer, reply.at[peer], arrived.at[:, mine], reply_send.at[peer], reply_recv.at[peer]
        ).wait_send()

    send_twin(0).wait_send()

    @pl.loop(1, pairs)
    def _(pair):
        send_twin(pair).wait_send()
        send_sum(pair, me, pair).wait_send()

    @pl.loop(0, lines)
    def _(back):
        @pl.when(back < lines - 1)
        def _():
            send_piece(me, holder(lines - 1, 0, 0), back * 4).wait_send()

        send_piece(me, holder(0, 1, 0), back * 4 + 1).wait_send()
        send_piece(me, holder(0, 0, 1), back * 4 + 2).wait_send()
        send_piece(me, holder(0, 0, 1), back * 4 + 3).wait_send()


def local(samples, centre_index, probe_signs, probe_scale):
    blocks = lax.axis_size("blk")
    features, s_dev = samples.shape
    m_dev = centre_index.shape[0]
    probes = probe_signs.shape[0]
    f32, bf16 = jnp.float32, jnp.bfloat16
    stored = min(blocks, STORE_BYTES // (s_dev * m_dev * 2)) // 2 * 2
    vmem = pl.BlockSpec(memory_space=pltpu.VMEM)
    return pl.pallas_call(
        functools.partial(body, blocks, stored),
        out_shape=jax.ShapeDtypeStruct((probes, m_dev), f32),
        in_specs=[vmem] * 4,
        out_specs=vmem,
        scratch_shapes=[
            pltpu.VMEM((s_dev, DEPTH), bf16),
            pltpu.VMEM((DEPTH, m_dev), bf16),
            pltpu.VMEM((probes, s_dev), f32),
            pltpu.VMEM((probes, s_dev), bf16),
            pltpu.VMEM((16 if blocks * LANES == s_dev else blocks * LANES, m_dev), bf16),
            pltpu.VMEM((blocks, 8, LANES), f32),
            pltpu.VMEM((blocks, 8, LANES), f32),
            pltpu.VMEM((blocks, features, LANES), bf16),
            pltpu.VMEM((features, blocks * LANES), bf16),
            pltpu.VMEM((blocks, features + probes, m_dev), bf16),
            pltpu.VMEM((stored + 1, s_dev, m_dev), bf16),
            pltpu.VMEM((blocks, probes, m_dev), bf16),
            pltpu.VMEM((blocks // 2, probes, m_dev), bf16),
            pltpu.VMEM((blocks // 2, probes, m_dev), bf16),
            pltpu.VMEM((probes, m_dev), f32),
        ] + [pltpu.SemaphoreType.DMA((blocks,))] * 10,
        compiler_params=pltpu.CompilerParams(
            collective_id=0, has_side_effects=True, vmem_limit_bytes=62 * 2**20
        ),
    )(samples, centre_index[None, :], probe_signs, probe_scale[None, :]).T


def solution(mesh):
    in_specs = (
        P(None, ("groups", "blk")),
        P(("groups", "blk")),
        P(None, ("groups", "blk")),
        P(("groups", "blk")),
    )
    out_specs = P(("groups", "blk"), None)
    return jax.shard_map(local, mesh=mesh, in_specs=in_specs, out_specs=out_specs, check_vma=False)
```
